32 devices in a mesh: clus: 8 (over z, y), rep: 4 (over x, core).
Axes of the slice: x: 2, y: 2, z: 4, core: 2. Of those that a mesh axis runs over, the one named last changes fastest.
Arguments:
- embeddings: bfloat16 [2048, 1024], P(('clus', 'rep')), may hold values from -700 to 700
- inv_temp: bfloat16 [2048], P(('clus', 'rep')), may hold values from 16 to 256
- routes: int32 [2048, 3], P(('clus', 'rep')), may hold values from 0 to 6, all different within a row; in each aligned block of 64 rows (0 to 63, 64 to 127, ...) at most 34 rows name the same one
Outputs:
- dup_score: float32 [2048], P(('clus', 'rep'))
The draws below stay inside these ranges and needn't reach their ends.
Inputs may be any that keep to these rules, and one draw needn't show every extreme that they name: `routes`: the values of one row are distinct. Within the rows of one device no value stands in more than 34 rows, and in some device one value stands in exactly 34 rows.
All inputs are finite; a program needn't handle non-finite values.
Results may differ from the reference program's by a relative error of at most 0.00051.
Values may be sent and summed in bfloat16 or wider, within the bound.
A program may use at most 64 MiB of HBM per device.

```python
import math
import jax
import jax.numpy as jnp
import numpy as np
from jax import lax

D = 1024
NB = 3
ROWS_DEV = 64
CLUSTER = 256
CLUSTERS = 8
TOKENS = 2048
MOST = 34
N_REP = 4


def draw_embeddings(key, part):
    key = jax.random.fold_in(key, 11)
    base_key, row_key, col_key = jax.random.split(key, 3)
    col_scale = jnp.exp(jax.random.uniform(col_key, (1, D), jnp.float32, 0.0, math.log(10.0)))
    row_scale = jnp.exp(jax.random.uniform(row_key, (TOKENS, 1), jnp.float32, 0.0, math.log(10.0)))
    base = jnp.clip(jax.random.normal(base_key, (TOKENS, D), jnp.float32), -6.0, 6.0)
    return (base * row_scale * col_scale).astype(jnp.bfloat16)


def level_of(key, dims, cuts, least, top_value):
    level, own = 1.0, jax.random.fold_in(key, 6)
    for dim, shards_of in cuts:
        heights = jnp.exp(jax.random.uniform(jax.random.fold_in(own, dim), (shards_of,), jnp.float32, least / len(cuts), top_value / len(cuts)))
        level = level * jnp.repeat(heights, dims[dim] // shards_of).reshape([-1 if axis == dim else 1 for axis in range(len(dims))])
    return level


def routed_block(rng, own, number, rows, count, top, most, skew):
    sequence = jax.random.permutation(rng, count)
    packed, ordinary = shares(count, rows * top, most, skew, True), shares(count, rows * top, most, skew, False)
    places = jnp.arange(count)

    def named(lengths, turn):
        used = int((lengths > 0).sum())
        fixed = max(1, used // 4)
        moved = fixed + (places - fixed + turn * (used - fixed)) % max(1, count - fixed)
        return jnp.zeros((count,), jnp.int32).at[sequence[jnp.where(places < fixed, places, moved)]].set(jnp.asarray(lengths, jnp.int32))

    lengths = jnp.where(number % 4 == 0, named(packed, number // 4), named(ordinary, number - number // 4 - 1))
    mixed = jax.random.permutation(jax.random.fold_in(own, 3), count)
    donor, taker = mixed[0:count // 2 * 2:2], mixed[1:count // 2 * 2:2]
    room = jnp.minimum(lengths[donor] - 1, most - lengths[taker]) // 2
    room = jnp.where((donor == sequence[0]) | (taker == sequence[0]) | (lengths[taker] == 0), 0, jnp.maximum(room, 0))
    moved = jax.random.randint(jax.random.fold_in(own, 4), (count // 2,), 0, 1 << 20) % (room + 1)
    lengths = lengths.at[donor].add(-moved).at[taker].add(moved)
    labels = jnp.searchsorted(jnp.cumsum(lengths), jnp.arange(rows * top), side="right").astype(jnp.int32)
    table = labels.reshape(top, rows).T
    table = table[jax.random.permutation(jax.random.fold_in(own, 1), rows)]
    turn = jax.random.randint(jax.random.fold_in(own, 2), (rows, 1), 0, top)
    return jnp.take_along_axis(table, (jnp.arange(top)[None, :] + turn) % top, axis=1)


def shares(count, total, most, slope, full):
    loads = [(1 << 20) // math.isqrt(rank ** slope) + 1 for rank in range(1, count + 1)]
    largest = most if full else min(most, max(-(-total // count), total * loads[0] // sum(loads)))
    least = 1 if total - largest >= count - 1 else 0
    given, spare = [largest] + [least] * (count - 1), total - largest - least * (count - 1)
    while spare > 0:
        candidates = [i for i in range(1, count) if given[i] < largest] or [i for i in range(1, count) if given[i] < most]
        mass, left = sum([loads[i] for i in candidates]), spare
        for i in candidates:
            extra = min(most - given[i], max(1, left * loads[i] // mass), spare)
            given[i] = given[i] + extra
            spare = spare - extra
    return np.array(given)


def setup_inputs(seed: int = 0) -> dict:
    splits = jax.random.split(jax.random.key(seed), 4)
    embeddings = draw_embeddings(jax.random.fold_in(splits[3], 71), 0)
    inv_temp = jnp.clip(jnp.exp(math.log(256.0) - 2.7725887 * jax.random.uniform(splits[1], (TOKENS,), jnp.float32) ** level_of(splits[1], (TOKENS,), ((0, 32),), -0.2, 0.2)), 16.0, 256.0).astype(jnp.bfloat16)
    routes_keys = jax.random.split(jax.random.fold_in(splits[2], 1), TOKENS // ROWS_DEV)
    routes_turns = jax.random.permutation(jax.random.fold_in(splits[2], 3), TOKENS // ROWS_DEV)
    routes = jax.vmap(lambda own, number: routed_block(jax.random.fold_in(splits[2], 2), own, number, ROWS_DEV, CLUSTERS - 1, NB, MOST, 2))(routes_keys, routes_turns).reshape((TOKENS, NB))
    return dict(embeddings=embeddings, inv_temp=inv_temp, routes=routes)


EPS = 1e-06

def unit_rows(values):
    widened = values.astype(jnp.float32)
    scale = lax.rsqrt(lax.optimization_barrier(jnp.sum(widened * widened, axis=1, keepdims=True)) + EPS)
    return (widened * scale).astype(jnp.bfloat16)

def row_stats(scores):
    top_score = lax.optimization_barrier(jnp.max(scores, axis=1))
    exp_mass = lax.optimization_barrier(jnp.sum(jnp.exp(scores - top_score[:, None]), axis=1))
    return (top_score, exp_mass)

def reference(embeddings, inv_temp, routes):
    normalized = unit_rows(embeddings)
    inverse = inv_temp.astype(jnp.float32)
    clusters = normalized.reshape(CLUSTERS, CLUSTER, D)
    inverse_blocks = inverse.reshape(CLUSTERS, CLUSTER)
    diagonal = jnp.eye(CLUSTER, dtype=jnp.bool_)

    def own_block(index):
        block = clusters[index].astype(jnp.float32)
        scores = jnp.dot(block, block.T, precision=lax.Precision.HIGHEST) * inverse_blocks[index][:, None]
        scores = jnp.where(diagonal, -jnp.inf, scores)
        return row_stats(scores)
    own_top, own_mass = lax.map(own_block, jnp.arange(CLUSTERS, dtype=jnp.int32))
    own_top = own_top.reshape(TOKENS)
    own_mass = own_mass.reshape(TOKENS)
    row_cluster = jnp.arange(TOKENS, dtype=jnp.int32) // CLUSTER
    targets = (row_cluster[:, None] + 1 + routes) % CLUSTERS
    flat_targets = targets.reshape(TOKENS * NB)
    bound = N_REP * CLUSTERS * MOST

    def near_block(index):
        picked = jnp.nonzero(flat_targets == index, size=bound, fill_value=TOKENS * NB)[0].astype(jnp.int32)
        query_rows = jnp.minimum(picked // NB, TOKENS - 1)
        block = normalized[query_rows].astype(jnp.float32)
        key_rows = clusters[index].astype(jnp.float32)
        scores = jnp.dot(block, key_rows.T, precision=lax.Precision.HIGHEST) * inverse[query_rows][:, None]
        top_score, exp_mass = row_stats(scores)
        return (picked, top_score, exp_mass)
    picked, top_score, exp_mass = lax.map(near_block, jnp.arange(CLUSTERS, dtype=jnp.int32))
    picked = picked.reshape(-1)
    near_top = jnp.zeros((TOKENS * NB,), jnp.float32).at[picked].set(top_score.reshape(-1), mode='drop').reshape(TOKENS, NB)
    near_mass = jnp.zeros((TOKENS * NB,), jnp.float32).at[picked].set(exp_mass.reshape(-1), mode='drop').reshape(TOKENS, NB)
    highest = jnp.maximum(own_top, lax.optimization_barrier(jnp.max(near_top, axis=1)))
    sum_total = own_mass * jnp.exp(own_top - highest) + lax.optimization_barrier(jnp.sum(near_mass * jnp.exp(near_top - highest[:, None]), axis=1))
    return (highest + jnp.log(sum_total)) / inverse
```

```python
import functools

import jax
import jax.numpy as jnp
from jax import lax
from jax.experimental import pallas as pl
from jax.experimental.pallas import tpu as pltpu
from jax.sharding import PartitionSpec as P

EPS = 1e-06


def unit_rows(values):
    widened = values.astype(jnp.float32)
    scale = lax.rsqrt(jnp.sum(widened * widened, axis=1, keepdims=True) + EPS)
    return (widened * scale).astype(jnp.bfloat16)


def block_stats(queries, inverse, key_rows, self_mask):
    scores = jnp.einsum("qd,kd->qk", queries, key_rows, preferred_element_type=jnp.float32)
    scores = scores * inverse.astype(jnp.float32)[:, None]
    if self_mask is not None:
        scores = jnp.where(self_mask, -jnp.inf, scores)
    top_score = jnp.max(scores, axis=1)
    exp_mass = jnp.sum(jnp.exp(scores - top_score[:, None]), axis=1)
    return (top_score, exp_mass)


def per_device(embeddings, inv_temp, routes):
    row_count, feature_width = embeddings.shape
    neighbours = routes.shape[1]
    owners = lax.axis_size("clus")
    replicas = lax.axis_size("rep")
    owner_self = lax.axis_index("clus")
    replica_self = lax.axis_index("rep")
    capacity = min(
        row_count,
        max(
            2,
            (row_count * neighbours + owners - 2) // (owners - 1)
            + row_count * neighbours // (4 * (owners - 1)),
        ),
    )
    normalized = unit_rows(embeddings)
    local_ids = jnp.arange(row_count, dtype=jnp.int32)
    cluster_ids = jnp.arange(row_count * replicas, dtype=jnp.int32)
    cluster_keys = lax.all_gather(normalized, "rep", axis=0, tiled=True)
    own_mask = cluster_ids[None, :] == (replica_self * row_count + local_ids)[:, None]
    own_top, own_mass = block_stats(normalized, inv_temp, cluster_keys, own_mask)
    targets = (owner_self + 1 + routes) % owners
    owner_ids = jnp.arange(owners, dtype=jnp.int32)
    target_hits = jnp.sum(
        (targets[:, :, None] == owner_ids[None, None, :]).astype(jnp.int32), axis=1
    )
    earlier_hits = jnp.cumsum(target_hits, axis=0) - target_hits
    slot_index = jnp.take_along_axis(earlier_hits, targets, axis=1)
    row_ids = jnp.broadcast_to(local_ids[:, None], targets.shape)
    source_table = jnp.zeros((owners, capacity), jnp.int32).at[targets, slot_index].set(row_ids)
    filled = (
        jnp.zeros((owners, capacity), jnp.bfloat16).at[targets, slot_index].set(jnp.bfloat16(1.0))
    )
    visitor_rows = normalized[source_table] * filled[:, :, None]
    visitor_inverse = inv_temp[source_table] * filled
    arrived = lax.all_to_all(visitor_rows, "clus", split_axis=0, concat_axis=0, tiled=True)
    arrived_inverse = lax.all_to_all(
        visitor_inverse, "clus", split_axis=0, concat_axis=0, tiled=True
    )
    senders = arrived.shape[0]
    item_count = arrived.shape[1]
    top_score, exp_mass = block_stats(
        arrived.reshape(senders * item_count, feature_width),
        arrived_inverse.reshape(senders * item_count),
        cluster_keys,
        None,
    )
    top_score = top_score.reshape(senders, item_count)
    exp_mass = exp_mass.reshape(senders, item_count)
    near_top = lax.all_to_all(top_score, "clus", split_axis=0, concat_axis=0, tiled=True)
    near_mass = lax.all_to_all(exp_mass, "clus", split_axis=0, concat_axis=0, tiled=True)
    picked_top = near_top[targets, slot_index]
    picked_mass = near_mass[targets, slot_index]
    highest = jnp.maximum(own_top, jnp.max(picked_top, axis=1))
    sum_total = own_mass * jnp.exp(own_top - highest) + jnp.sum(
        picked_mass * jnp.exp(picked_top - highest[:, None]), axis=1
    )
    return (highest + jnp.log(sum_total)) / inv_temp.astype(jnp.float32)


NEG = float("-inf")
RING = (0, 3, 5, 4, 1, 6, 7, 2)


def lookup(table, index):
    value = jnp.int32(table[0])
    for place in range(1, len(table)):
        value = jnp.where(index == place, jnp.int32(table[place]), value)
    return value


def dot_nt(left, right):
    return lax.dot_general(
        left, right, (((1,), (1,)), ((), ())), preferred_element_type=jnp.float32
    )


def column_stats(scores):
    top = jnp.max(scores, axis=0, keepdims=True)
    return top, jnp.sum(jnp.exp(scores - top), axis=0, keepdims=True)


def meet_kernel(
    owners, replicas,
    emb_ref, inv_ref, routes_ref, out_ref,
    keys, key_inv, guests, guest_inv, reply, replied, part, parts,
    key_send, key_recv, kinv_send, kinv_recv, guest_send, guest_recv,
    ginv_send, ginv_recv, reply_send, reply_recv, part_send, part_recv,
):
    rows = emb_ref.shape[0]
    half = owners // 2
    cluster = lax.axis_index("clus")
    rep = lax.axis_index("rep")
    ring = RING
    place_of = tuple(ring.index(c) for c in range(owners))
    place = lookup(place_of, cluster)
    at = [lookup(ring, lax.rem(place + step, owners)) for step in range(owners)]
    gives = place >= half
    peers = [lax.rem(rep + step, replicas) for step in range(replicas)]

    barrier = pltpu.get_barrier_semaphore()
    for step in range(1, owners):
        pl.semaphore_signal(barrier, inc=1, device_id=(at[step], rep), device_id_type=pl.DeviceIdType.MESH)
    for step in range(1, replicas):
        pl.semaphore_signal(barrier, inc=1, device_id=(cluster, peers[step]), device_id_type=pl.DeviceIdType.MESH)

    widened = emb_ref[...].astype(jnp.float32)
    scale = lax.rsqrt(jnp.sum(widened * widened, axis=1, keepdims=True) + EPS)
    unit = (widened * scale).astype(jnp.bfloat16)
    keys[rep] = unit
    spread = (
        lax.broadcasted_iota(jnp.int32, (rows, 2 * rows), 0)
        == lax.rem(lax.broadcasted_iota(jnp.int32, (rows, 2 * rows), 1), rows)
    ).astype(jnp.bfloat16)
    inv_row = jnp.dot(
        jnp.broadcast_to(inv_ref[...], (16, rows)), spread, preferred_element_type=jnp.float32
    )[0:8]
    key_inv[rep] = inv_row
    inverse = inv_row[0:1, 0:rows]
    reply[...] = jnp.zeros_like(reply)
    part[...] = jnp.zeros_like(part)

    def remote(source, target, send, recv, device):
        return pltpu.make_async_remote_copy(
            src_ref=source, dst_ref=target, send_sem=send, recv_sem=recv,
            device_id=device, device_id_type=pl.DeviceIdType.MESH,
        )

    key_copies, kinv_copies, part_copies = [], [], []
    for step in range(1, replicas):
        device = (cluster, peers[step])
        key_copies.append(remote(keys.at[rep], keys.at[rep], key_send.at[step - 1], key_recv.at[step - 1], device))
        kinv_copies.append(remote(key_inv.at[rep], key_inv.at[rep], kinv_send.at[step - 1], kinv_recv.at[step - 1], device))
        part_copies.append(remote(part, parts.at[rep], part_send.at[step - 1], part_recv.at[step - 1], device))
    guest_copies, ginv_copies, reply_copies = [], [], []
    for step in range(1, half + 1):
        slot = step - 1
        device = (at[step], rep)
        guest_copies.append(remote(keys.at[rep], guests.at[slot], guest_send.at[slot], guest_recv.at[slot], device))
        ginv_copies.append(remote(key_inv.at[rep], guest_inv.at[slot], ginv_send.at[slot], ginv_recv.at[slot], device))
        back = (at[owners - step], rep)
        reply_copies.append(remote(reply.at[slot], replied.at[slot], reply_send.at[slot], reply_recv.at[slot], back))

    pl.semaphore_wait(barrier, owners - 1 + replicas - 1)
    for copy in kinv_copies:
        copy.start()
    for slot in range(half - 1):
        ginv_copies[slot].start()
    for slot in range(max(half - 1, replicas - 1)):
        if slot < half - 1:
            guest_copies[slot].start()
        if slot < replicas - 1:
            key_copies[slot].start()

    @pl.when(gives)
    def _():
        ginv_copies[half - 1].start()
        guest_copies[half - 1].start()

    diagonal = (
        lax.broadcasted_iota(jnp.int32, (rows, rows), 0)
        == lax.broadcasted_iota(jnp.int32, (rows, rows), 1)
    )
    routes = routes_ref[...]
    turned = [
        jnp.sum(jnp.where(diagonal, routes[:, k : k + 1], 0), axis=0, keepdims=True)
        for k in range(routes.shape[1])
    ]
    hits = [None]
    for step in range(1, owners):
        wanted = lax.rem(at[step] - cluster - 1 + owners, owners)
        hit = turned[0] == wanted
        for other in turned[1:]:
            hit = hit | (other == wanted)
        hits.append(hit)

    for copy in kinv_copies + key_copies:
        copy.wait_recv()
    cluster_rows = keys[...].reshape(replicas * rows, keys.shape[2])
    lane = lax.broadcasted_iota(jnp.int32, (1, 2 * rows), 1)
    cluster_inv = jnp.concatenate(
        [
            jnp.where(lane < rows, key_inv[2 * pair][0:1], key_inv[2 * pair + 1][0:1])
            for pair in range(replicas // 2)
        ],
        axis=1,
    )
    own = dot_nt(cluster_rows, keys[rep]) * inverse
    own = jnp.where(
        lax.broadcasted_iota(jnp.int32, own.shape, 0)
        == rep * rows + lax.broadcasted_iota(jnp.int32, own.shape, 1),
        NEG,
        own,
    )
    own_top, own_mass = column_stats(own)

    def meet(slot):
        ginv_copies[slot].wait_recv()
        guest_copies[slot].wait_recv()
        guest = guests[slot]
        top, mass = column_stats(dot_nt(cluster_rows, guest) * guest_inv[slot][0:1, 0:rows])
        reply[slot, 0:1, 0:rows] = top
        reply[slot, 1:2, 0:rows] = mass
        reply_copies[slot].start()
        top, mass = column_stats(dot_nt(guest, cluster_rows) * cluster_inv)
        part[slot : slot + 1, :] = top
        part[half + slot : half + slot + 1, :] = mass

    for slot in range(half - 1):
        meet(slot)

    @pl.when(jnp.logical_not(gives))
    def _():
        meet(half - 1)

    for copy in part_copies:
        copy.start()
    parts[rep] = part[...]

    for slot in range(half - 1):
        reply_copies[slot].wait_recv()

    @pl.when(gives)
    def _():
        reply_copies[half - 1].wait_recv()

    for copy in part_copies:
        copy.wait_recv()

    pieces = []
    for other in range(replicas):
        whole = parts[other]
        piece = whole[:, 0 : 2 * rows]
        for pair in range(1, replicas // 2):
            piece = jnp.where(rep // 2 == pair, whole[:, 2 * rows * pair : 2 * rows * (pair + 1)], piece)
        piece = jnp.where(rep % 2 == 1, pltpu.roll(piece, rows, 1), piece)
        pieces.append(piece[:, 0:rows])
    part_top = functools.reduce(jnp.maximum, [piece[0:half] for piece in pieces])
    part_mass = sum(piece[half : 2 * half] * jnp.exp(piece[0:half] - part_top) for piece in pieces)

    found = []
    for step in range(1, half):
        found.append((hits[step], replied[step - 1, 0:1, 0:rows], replied[step - 1, 1:2, 0:rows]))
        found.append((hits[owners - step], part_top[step - 1 : step], part_mass[step - 1 : step]))
    found.append((
        hits[half],
        jnp.where(gives, replied[half - 1, 0:1, 0:rows], part_top[half - 1 : half]),
        jnp.where(gives, replied[half - 1, 1:2, 0:rows], part_mass[half - 1 : half]),
    ))
    highest = own_top
    for hit, top, _ in found:
        highest = jnp.maximum(highest, jnp.where(hit, top, NEG))
    total = own_mass * jnp.exp(own_top - highest)
    for hit, top, mass in found:
        total += jnp.where(hit, mass * jnp.exp(top - highest), 0.0)
    out_ref[...] = (highest + jnp.log(total)) / inverse

    for copy in key_copies + kinv_copies + part_copies:
        copy.wait_send()
    for slot in range(half - 1):
        ginv_copies[slot].wait_send()
        guest_copies[slot].wait_send()
        reply_copies[slot].wait_send()

    @pl.when(gives)
    def _():
        ginv_copies[half - 1].wait_send()
        guest_copies[half - 1].wait_send()

    @pl.when(jnp.logical_not(gives))
    def _():
        reply_copies[half - 1].wait_send()


def meet_per_device(owners, replicas, embeddings, inv_temp, routes):
    rows, width = embeddings.shape
    half = owners // 2
    vmem = pl.BlockSpec(memory_space=pltpu.VMEM)
    dma = pltpu.SemaphoreType.DMA
    result = pl.pallas_call(
        functools.partial(meet_kernel, owners, replicas),
        out_shape=jax.ShapeDtypeStruct((1, rows), jnp.float32),
        in_specs=[vmem] * 3,
        out_specs=vmem,
        scratch_shapes=[
            pltpu.VMEM((replicas, rows, width), jnp.bfloat16),
            pltpu.VMEM((replicas, 8, 2 * rows), jnp.float32),
            pltpu.VMEM((half, rows, width), jnp.bfloat16),
            pltpu.VMEM((half, 8, 2 * rows), jnp.float32),
            pltpu.VMEM((half, 8, 2 * rows), jnp.float32),
            pltpu.VMEM((half, 8, 2 * rows), jnp.float32),
            pltpu.VMEM((2 * half, replicas * rows), jnp.float32),
            pltpu.VMEM((replicas, 2 * half, replicas * rows), jnp.float32),
        ]
        + [dma((replicas - 1,))] * 4
        + [dma((half,))] * 6
        + [dma((replicas - 1,))] * 2,
        compiler_params=pltpu.CompilerParams(
            collective_id=0, has_side_effects=True, vmem_limit_bytes=32 * 1024 * 1024
        ),
    )(embeddings, inv_temp.reshape(1, rows), routes)
    return result.reshape(rows)


def solution(mesh):
    in_specs = (P(("clus", "rep"), None), P(("clus", "rep")), P(("clus", "rep"), None))
    out_specs = P(("clus", "rep"))
    owners, replicas = mesh.shape["clus"], mesh.shape["rep"]
    body = per_device
    if owners == len(RING) and replicas == 4:
        body = functools.partial(meet_per_device, owners, replicas)
    return jax.shard_map(
        body, mesh=mesh, in_specs=in_specs, out_specs=out_specs, check_vma=False
    )
```

```python
import functools

import jax
import jax.numpy as jnp
from jax import lax
from jax.experimental import pallas as pl
from jax.experimental.pallas import tpu as pltpu
from jax.sharding import PartitionSpec as P

EPS = 1e-06


def unit_rows(values):
    widened = values.astype(jnp.float32)
    scale = lax.rsqrt(jnp.sum(widened * widened, axis=1, keepdims=True) + EPS)
    return (widened * scale).astype(jnp.bfloat16)


def block_stats(queries, inverse, key_rows, self_mask):
    scores = jnp.einsum("qd,kd->qk", queries, key_rows, preferred_element_type=jnp.float32)
    scores = scores * inverse.astype(jnp.float32)[:, None]
    if self_mask is not None:
        scores = jnp.where(self_mask, -jnp.inf, scores)
    top_score = jnp.max(scores, axis=1)
    exp_mass = jnp.sum(jnp.exp(scores - top_score[:, None]), axis=1)
    return (top_score, exp_mass)


def per_device(embeddings, inv_temp, routes):
    row_count, feature_width = embeddings.shape
    neighbours = routes.shape[1]
    owners = lax.axis_size("clus")
    replicas = lax.axis_size("rep")
    owner_self = lax.axis_index("clus")
    replica_self = lax.axis_index("rep")
    capacity = min(
        row_count,
        max(
            2,
            (row_count * neighbours + owners - 2) // (owners - 1)
            + row_count * neighbours // (4 * (owners - 1)),
        ),
    )
    normalized = unit_rows(embeddings)
    local_ids = jnp.arange(row_count, dtype=jnp.int32)
    cluster_ids = jnp.arange(row_count * replicas, dtype=jnp.int32)
    cluster_keys = lax.all_gather(normalized, "rep", axis=0, tiled=True)
    own_mask = cluster_ids[None, :] == (replica_self * row_count + local_ids)[:, None]
    own_top, own_mass = block_stats(normalized, inv_temp, cluster_keys, own_mask)
    targets = (owner_self + 1 + routes) % owners
    owner_ids = jnp.arange(owners, dtype=jnp.int32)
    target_hits = jnp.sum(
        (targets[:, :, None] == owner_ids[None, None, :]).astype(jnp.int32), axis=1
    )
    earlier_hits = jnp.cumsum(target_hits, axis=0) - target_hits
    slot_index = jnp.take_along_axis(earlier_hits, targets, axis=1)
    row_ids = jnp.broadcast_to(local_ids[:, None], targets.shape)
    source_table = jnp.zeros((owners, capacity), jnp.int32).at[targets, slot_index].set(row_ids)
    filled = (
        jnp.zeros((owners, capacity), jnp.bfloat16).at[targets, slot_index].set(jnp.bfloat16(1.0))
    )
    visitor_rows = normalized[source_table] * filled[:, :, None]
    visitor_inverse = inv_temp[source_table] * filled
    arrived = lax.all_to_all(visitor_rows, "clus", split_axis=0, concat_axis=0, tiled=True)
    arrived_inverse = lax.all_to_all(
        visitor_inverse, "clus", split_axis=0, concat_axis=0, tiled=True
    )
    senders = arrived.shape[0]
    item_count = arrived.shape[1]
    top_score, exp_mass = block_stats(
        arrived.reshape(senders * item_count, feature_width),
        arrived_inverse.reshape(senders * item_count),
        cluster_keys,
        None,
    )
    top_score = top_score.reshape(senders, item_count)
    exp_mass = exp_mass.reshape(senders, item_count)
    near_top = lax.all_to_all(top_score, "clus", split_axis=0, concat_axis=0, tiled=True)
    near_mass = lax.all_to_all(exp_mass, "clus", split_axis=0, concat_axis=0, tiled=True)
    picked_top = near_top[targets, slot_index]
    picked_mass = near_mass[targets, slot_index]
    highest = jnp.maximum(own_top, jnp.max(picked_top, axis=1))
    sum_total = own_mass * jnp.exp(own_top - highest) + jnp.sum(
        picked_mass * jnp.exp(picked_top - highest[:, None]), axis=1
    )
    return (highest + jnp.log(sum_total)) / inv_temp.astype(jnp.float32)


NEG = float("-inf")
RING = (0, 4, 1, 5, 2, 6, 3, 7)
GIVERS = (1, 0, 1, 0, 0, 1, 0, 1)
PIECES = 4


def lookup(table, index):
    value = jnp.int32(table[0])
    for place in range(1, len(table)):
        value = jnp.where(index == place, jnp.int32(table[place]), value)
    return value


def dot_nt(left, right):
    return lax.dot_general(
        left, right, (((1,), (1,)), ((), ())), preferred_element_type=jnp.float32
    )


def column_stats(scores):
    top = jnp.max(scores, axis=0, keepdims=True)
    return top, jnp.sum(jnp.exp(scores - top), axis=0, keepdims=True)


def meet_kernel(
    owners, replicas,
    emb_hbm, inv_hbm, routes_hbm, out_ref, emb_ref, inv_ref, routes_ref,
    keys, key_inv, guests, guest_inv, reply, replied, part, parts,
    key_send, key_recv, kinv_send, kinv_recv, guest_send, guest_recv,
    ginv_send, ginv_recv, reply_send, reply_recv, part_send, part_recv, fetch_sem,
):
    rows = emb_ref.shape[0]
    fetches = [
        pltpu.make_async_copy(source, target, fetch_sem.at[k])
        for k, (source, target) in enumerate(
            ((emb_hbm, emb_ref), (inv_hbm, inv_ref), (routes_hbm, routes_ref))
        )
    ]
    for fetch in fetches:
        fetch.start()
    half = owners // 2
    cluster = lax.axis_index("clus")
    rep = lax.axis_index("rep")
    ring = RING
    place_of = tuple(ring.index(c) for c in range(owners))
    place = lookup(place_of, cluster)
    at = [lookup(ring, lax.rem(place + step, owners)) for step in range(owners)]
    gives = lookup(GIVERS, place) == 1
    hands = lookup(GIVERS, lax.rem(place + owners - 1, owners)) == 1
    peers = [lax.rem(rep + step, replicas) for step in range(replicas)]

    barrier = pltpu.get_barrier_semaphore()
    for step in range(1, owners):
        pl.semaphore_signal(barrier, inc=1, device_id=(at[step], rep), device_id_type=pl.DeviceIdType.MESH)
    for step in range(1, replicas):
        pl.semaphore_signal(barrier, inc=1, device_id=(cluster, peers[step]), device_id_type=pl.DeviceIdType.MESH)

    for fetch in fetches:
        fetch.wait()
    widened = emb_ref[...].astype(jnp.float32)
    scale = lax.rsqrt(jnp.sum(widened * widened, axis=1, keepdims=True) + EPS)
    unit = (widened * scale).astype(jnp.bfloat16)
    keys[rep] = unit
    spread = (
        lax.broadcasted_iota(jnp.int32, (rows, 2 * rows), 0)
        == lax.rem(lax.broadcasted_iota(jnp.int32, (rows, 2 * rows), 1), rows)
    ).astype(jnp.bfloat16)
    inv_row = jnp.dot(
        jnp.broadcast_to(inv_ref[...], (16, rows)), spread, preferred_element_type=jnp.float32
    )[0:8]
    key_inv[rep] = inv_row
    inverse = inv_row[0:1, 0:rows]
    reply[...] = jnp.zeros_like(reply)
    part[...] = jnp.zeros_like(part)

    def remote(source, target, send, recv, device):
        return pltpu.make_async_remote_copy(
            src_ref=source, dst_ref=target, send_sem=send, recv_sem=recv,
            device_id=device, device_id_type=pl.DeviceIdType.MESH,
        )

    key_copies, kinv_copies, part_copies = [], [], []
    for step in range(1, replicas):
        device = (cluster, peers[step])
        key_copies.append(remote(keys.at[rep], keys.at[rep], key_send.at[step - 1], key_recv.at[step - 1], device))
        kinv_copies.append(remote(key_inv.at[rep], key_inv.at[rep], kinv_send.at[step - 1], kinv_recv.at[step - 1], device))
        part_copies.append(remote(part, parts.at[rep], part_send.at[step - 1], part_recv.at[step - 1], device))
    size = rows // PIECES
    guest_copies, ginv_copies, reply_copies = [], [], []
    for step in range(1, half + 1):
        slot = step - 1
        device = (at[step], rep)
        relayed = step > 2
        target = (at[step - 1], rep) if relayed else device
        origin = guests.at[0] if relayed else keys.at[rep]
        guest_copies.append([
            remote(
                origin.at[pl.ds(piece * size, size)], guests.at[slot, pl.ds(piece * size, size)],
                guest_send.at[slot, piece], guest_recv.at[slot, piece], target,
            )
            for piece in range(PIECES)
        ])
        ginv_copies.append(remote(key_inv.at[rep], guest_inv.at[slot], ginv_send.at[slot], ginv_recv.at[slot], device))
        back = (at[owners - step], rep)
        reply_copies.append(remote(reply.at[slot], replied.at[slot], reply_send.at[slot], reply_recv.at[slot], back))

    pl.semaphore_wait(barrier, owners - 1 + replicas - 1)
    for copy in guest_copies[0]:
        copy.start()
    for copy in kinv_copies:
        copy.start()
    for copy in key_copies:
        copy.start()
    for copy in guest_copies[1]:
        copy.start()
    for slot in range(half - 1):
        ginv_copies[slot].start()

    @pl.when(gives)
    def _():
        ginv_copies[half - 1].start()

    routes = routes_ref[...]
    turned = [routes[k : k + 1] for k in range(routes.shape[0])]
    hits = [None]
    for step in range(1, owners):
        wanted = lax.rem(at[step] - cluster - 1 + owners, owners)
        hit = turned[0] == wanted
        for other in turned[1:]:
            hit = hit | (other == wanted)
        hits.append(hit)

    for piece in range(PIECES):
        guest_copies[0][piece].wait_recv()
        guest_copies[2][piece].start()

        @pl.when(hands)
        def _():
            guest_copies[3][piece].start()

    for copy in kinv_copies + key_copies:
        copy.wait_recv()
    cluster_rows = keys[...].reshape(replicas * rows, keys.shape[2])
    lane = lax.broadcasted_iota(jnp.int32, (1, 2 * rows), 1)
    cluster_inv = jnp.concatenate(
        [
            jnp.where(lane < rows, key_inv[2 * pair][0:1], key_inv[2 * pair + 1][0:1])
            for pair in range(replicas // 2)
        ],
        axis=1,
    )
    own = dot_nt(cluster_rows, keys[rep]) * inverse
    own = jnp.where(
        lax.broadcasted_iota(jnp.int32, own.shape, 0)
        == rep * rows + lax.broadcasted_iota(jnp.int32, own.shape, 1),
        NEG,
        own,
    )
    own_top, own_mass = column_stats(own)

    def meet(slot):
        ginv_copies[slot].wait_recv()
        if slot > 0:
            for copy in guest_copies[slot]:
                copy.wait_recv()
        guest = guests[slot]
        top, mass = column_stats(dot_nt(cluster_rows, guest) * guest_inv[slot][0:1, 0:rows])
        reply[slot, 0:1, 0:rows] = top
        reply[slot, 1:2, 0:rows] = mass
        reply_copies[slot].start()
        top, mass = column_stats(dot_nt(guest, cluster_rows) * cluster_inv)
        part[slot : slot + 1, :] = top
        part[half + slot : half + slot + 1, :] = mass

    for slot in range(half - 1):
        meet(slot)

    @pl.when(jnp.logical_not(gives))
    def _():
        meet(half - 1)

    for copy in part_copies:
        copy.start()
    parts[rep] = part[...]

    for slot in range(half - 1):
        reply_copies[slot].wait_recv()

    @pl.when(gives)
    def _():
        reply_copies[half - 1].wait_recv()

    for copy in part_copies:
        copy.wait_recv()

    pieces = []
    for other in range(replicas):
        whole = parts[other]
        piece = whole[:, 0 : 2 * rows]
        for pair in range(1, replicas // 2):
            piece = jnp.where(rep // 2 == pair, whole[:, 2 * rows * pair : 2 * rows * (pair + 1)], piece)
        piece = jnp.where(rep % 2 == 1, pltpu.roll(piece, rows, 1), piece)
        pieces.append(piece[:, 0:rows])
    part_top = functools.reduce(jnp.maximum, [piece[0:half] for piece in pieces])
    part_mass = sum(piece[half : 2 * half] * jnp.exp(piece[0:half] - part_top) for piece in pieces)

    found = []
    for step in range(1, half):
        found.append((hits[step], replied[step - 1, 0:1, 0:rows], replied[step - 1, 1:2, 0:rows]))
        found.append((hits[owners - step], part_top[step - 1 : step], part_mass[step - 1 : step]))
    found.append((
        hits[half],
        jnp.where(gives, replied[half - 1, 0:1, 0:rows], part_top[half - 1 : half]),
        jnp.where(gives, replied[half - 1, 1:2, 0:rows], part_mass[half - 1 : half]),
    ))
    highest = own_top
    for hit, top, _ in found:
        highest = jnp.maximum(highest, jnp.where(hit, top, NEG))
    total = own_mass * jnp.exp(own_top - highest)
    for hit, top, mass in found:
        total += jnp.where(hit, mass * jnp.exp(top - highest), 0.0)
    out_ref[...] = (highest + jnp.log(total)) / inverse

    for copy in key_copies + kinv_copies + part_copies:
        copy.wait_send()
    for slot in range(half - 1):
        ginv_copies[slot].wait_send()
        reply_copies[slot].wait_send()
        for copy in guest_copies[slot]:
            copy.wait_send()

    @pl.when(hands)
    def _():
        for copy in guest_copies[half - 1]:
            copy.wait_send()

    @pl.when(gives)
    def _():
        ginv_copies[half - 1].wait_send()

    @pl.when(jnp.logical_not(gives))
    def _():
        reply_copies[half - 1].wait_send()


def meet_per_device(owners, replicas, embeddings, inv_temp, routes):
    rows, width = embeddings.shape
    half = owners // 2
    vmem = pl.BlockSpec(memory_space=pltpu.VMEM)
    dma = pltpu.SemaphoreType.DMA
    result = pl.pallas_call(
        functools.partial(meet_kernel, owners, replicas),
        out_shape=jax.ShapeDtypeStruct((1, rows), jnp.float32),
        in_specs=[pl.BlockSpec(memory_space=pl.ANY)] * 3,
        out_specs=vmem,
        scratch_shapes=[
            pltpu.VMEM((rows, width), jnp.bfloat16),
            pltpu.VMEM((1, rows), inv_temp.dtype),
            pltpu.VMEM((routes.shape[1], rows), routes.dtype),
            pltpu.VMEM((replicas, rows, width), jnp.bfloat16),
            pltpu.VMEM((replicas, 8, 2 * rows), jnp.float32),
            pltpu.VMEM((half, rows, width), jnp.bfloat16),
            pltpu.VMEM((half, 8, 2 * rows), jnp.float32),
            pltpu.VMEM((half, 8, 2 * rows), jnp.float32),
            pltpu.VMEM((half, 8, 2 * rows), jnp.float32),
            pltpu.VMEM((2 * half, replicas * rows), jnp.float32),
            pltpu.VMEM((replicas, 2 * half, replicas * rows), jnp.float32),
        ]
        + [dma((replicas - 1,))] * 4
        + [dma((half, PIECES))] * 2
        + [dma((half,))] * 4
        + [dma((replicas - 1,))] * 2
        + [dma((3,))],
        compiler_params=pltpu.CompilerParams(
            collective_id=0, has_side_effects=True, vmem_limit_bytes=60 * 1024 * 1024
        ),
    )(embeddings, inv_temp.reshape(1, rows), routes.T)
    return result.reshape(rows)


def solution(mesh):
    in_specs = (P(("clus", "rep"), None), P(("clus", "rep")), P(("clus", "rep"), None))
    out_specs = P(("clus", "rep"))
    owners, replicas = mesh.shape["clus"], mesh.shape["rep"]
    body = per_device
    if owners == len(RING) and replicas == 4:
        body = functools.partial(meet_per_device, owners, replicas)
    return jax.shard_map(
        body, mesh=mesh, in_specs=in_specs, out_specs=out_specs, check_vma=False
    )
```
